128 devices in a mesh: user: 32 (over y, x, core), item: 4 (over z).
Axes of the slice: x: 4, y: 4, z: 4, core: 2. Of those that a mesh axis runs over, the one named last changes fastest.
Arguments:
- user_factors: float32 [16384, 256], P('user'), may hold values from -1.5 to 1.5
- item_factors: float32 [131072, 256], P(('user', 'item')), may hold values from -1.5 to 1.5
- feedback: bfloat16 [512, 16384, 128], P('item', 'user'), may hold values from 0 to 1
- item_pick: int32 [128, 128], replicated, may hold values from 0 to 7, as said below
- user_noise: float32 [16384, 256], P('user'), may hold values from -6 to 6
- item_noise: float32 [131072, 256], P(('user', 'item')), may hold values from -6 to 6
Outputs:
- new_user: float32 [16384, 256], P('user')
- new_item: float32 [131072, 256], P(('user', 'item'))
The draws below stay inside these ranges and needn't reach their ends.
Inputs may be any that keep to these rules, and one draw needn't show every extreme that they name: For every owner o and every user slab u, the 4 entries item_pick[u * 4 + i, o] are distinct, so that no tile appears twice.
All inputs are finite; a program needn't handle non-finite values.
Results may differ from the reference program's by a relative error of at most 0.00058.
Values may be sent and summed in bfloat16 or wider, within the bound.
No kernel may reach another device: no remote copies, remote signals or barrier semaphores. Data moves between devices by JAX's collectives and lax.ppermute only.
A program may use at most 192 MiB of HBM per device.

```python
import math
import jax
import jax.numpy as jnp
from jax import lax

RANK = 256
TILE = 128
UB_DEV = 4
IB_DEV = 8
USERS = 16384
ITEMS = 131072
N_ITEM = 4
DEVICES = 128


def draw_item_pick(key, part):
    user_rows = DEVICES // N_ITEM
    ranking = jax.random.randint(key, (user_rows, DEVICES, IB_DEV), 0, 1 << 20) * IB_DEV + jnp.arange(IB_DEV, dtype=jnp.int32)
    picked = jnp.argsort(ranking, axis=-1)[:, :, :N_ITEM]
    return jnp.transpose(picked, (0, 2, 1)).reshape(DEVICES, DEVICES).astype(jnp.int32)


def level_of(own_key, dims, split, smallest, largest):
    def one(axis_at, shards_of):
        draws = jax.random.uniform(jax.random.fold_in(jax.random.fold_in(own_key, 6), axis_at), (shards_of,), jnp.float32, smallest / len(split), largest / len(split))
        return jnp.repeat(jnp.exp(draws), dims[axis_at] // shards_of).reshape((-1,) + (1,) * (len(dims) - axis_at - 1))

    factor_of = one(*split[0])
    for cut in split[1:]:
        factor_of = factor_of * one(*cut)
    return factor_of


def scatter_about(own_key, shape, deviation, reach, shards=(), kind=jnp.bfloat16):
    loudness = level_of(own_key, shape, shards, -0.22, 0.18) if shards else 1.0
    values = jax.random.normal(own_key, shape, jnp.float32) * deviation * loudness
    return jnp.minimum(jnp.maximum(values, -reach), reach).astype(kind)


def setup_inputs(seed: int = 0) -> dict:
    key_of = jax.random.split(jax.random.key(seed), 7)
    user_factors = scatter_about(key_of[0], (USERS, RANK), 0.25, 1.5, ((0, 32),), jnp.float32)
    item_factors = scatter_about(key_of[1], (ITEMS, RANK), 0.25, 1.5, ((0, 128),), jnp.float32)
    feedback = jnp.clip(1.0 * jax.random.uniform(key_of[2], (N_ITEM * DEVICES, USERS, TILE), jnp.float32) ** level_of(key_of[2], (N_ITEM * DEVICES, USERS, TILE), ((0, 4), (1, 32)), -0.2, 0.2), 0.0, 1.0).astype(jnp.bfloat16)
    item_pick = draw_item_pick(jax.random.fold_in(key_of[6], 71), 0)
    user_noise = scatter_about(key_of[4], (USERS, RANK), 1.0, 6.0, ((0, 32),), jnp.float32)
    item_noise = scatter_about(key_of[5], (ITEMS, RANK), 1.0, 6.0, ((0, 128),), jnp.float32)
    return {"user_factors": user_factors, "item_factors": item_factors, "feedback": feedback, "item_pick": item_pick, "user_noise": user_noise, "item_noise": item_noise}


step_size = 0.01
item_step = 0.1
prior_weight = 1.0
noise_scale = math.sqrt(0.02)
item_noise_scale = math.sqrt(0.2)

def reference(user_factors, item_factors, feedback, item_pick, user_noise, item_noise):
    slab_rows = UB_DEV * TILE
    item_half = item_factors.astype(jnp.bfloat16).reshape(IB_DEV * DEVICES, TILE, RANK)
    owners = jnp.arange(DEVICES, dtype=jnp.int32) * IB_DEV

    def one_device(totals, device):
        user_row = (device // N_ITEM).astype(jnp.int32)
        item_col = (device % N_ITEM).astype(jnp.int32)
        user_slab = lax.dynamic_slice_in_dim(user_factors, user_row * slab_rows, slab_rows, 0).astype(jnp.bfloat16)
        tiles = lax.dynamic_slice(feedback, (item_col * DEVICES, user_row * slab_rows, jnp.int32(0)), (DEVICES, slab_rows, TILE))
        blocks = (owners + item_pick[device]).astype(jnp.int32)
        fetched = item_half[blocks]
        scores = jnp.einsum('uk,ntk->nut', user_slab.astype(jnp.float32), fetched.astype(jnp.float32))
        residual = (jax.nn.sigmoid(scores) - tiles.astype(jnp.float32)).astype(jnp.bfloat16)
        user_grad = jnp.einsum('nut,ntk->uk', residual.astype(jnp.float32), fetched.astype(jnp.float32))
        item_part = jnp.einsum('nut,uk->ntk', residual.astype(jnp.float32), user_slab.astype(jnp.float32))
        totals = totals.at[blocks].add(item_part)
        return (totals, user_grad)
    start_grad = jnp.zeros((IB_DEV * DEVICES, TILE, RANK), jnp.float32)
    item_grad, user_parts = lax.scan(one_device, start_grad, jnp.arange(DEVICES, dtype=jnp.int32))
    user_grad = lax.optimization_barrier(jnp.sum(user_parts.reshape(DEVICES // N_ITEM, N_ITEM, slab_rows, RANK), axis=1)).reshape(USERS, RANK)
    new_user = user_factors - step_size * (user_grad + prior_weight * user_factors) + noise_scale * user_noise
    new_item = item_factors - item_step * (item_grad.reshape(ITEMS, RANK) + prior_weight * item_factors) + item_noise_scale * item_noise
    return (new_user, new_item)
```

```python
import functools
import math

import jax
import jax.numpy as jnp
from jax import lax
from jax.experimental import pallas as pl
from jax.experimental.pallas import tpu as pltpu
from jax.sharding import PartitionSpec as P

step_size = 0.01
item_step = 0.1
prior_weight = 1.0
noise_scale = math.sqrt(0.02)
item_noise_scale = math.sqrt(0.2)

PARTS = 2
VMEM_LIMIT = 60 * 1024 * 1024
AXES = ("user", "item")

CODE_FLOOR = 2.0**-20
CODE_RATE = 32700.0 / math.log2(1.0 + 776.0 / CODE_FLOOR)


def encode(part):
    level = jnp.log2(1.0 + jnp.abs(part) * (1.0 / CODE_FLOOR)) * CODE_RATE + 0.5
    level = level.astype(jnp.int32)
    return jnp.where(part < 0.0, -level, level).astype(jnp.int16)


def decode(code):
    code = code.astype(jnp.float32)
    size = jnp.exp2(jnp.abs(code) * (1.0 / CODE_RATE)) * CODE_FLOOR - CODE_FLOOR
    return jnp.where(code < 0.0, -size, size)


def pack_kernel(per_step, rows, wanted_ref, seg_ref, item_ref, out_ref):
    step = pl.program_id(0)
    start = pl.multiple_of(seg_ref[0] * rows, rows)
    for j in range(per_step):
        block = wanted_ref[step * per_step + j]
        out_ref[j] = item_ref[block, pl.ds(start, rows), :].astype(jnp.bfloat16)


def pack(item_blocks, wanted, seg, rows):
    held, tile, rank = item_blocks.shape
    count = wanted.shape[0]
    per_step = 16
    return pl.pallas_call(
        functools.partial(pack_kernel, per_step, rows),
        out_shape=jax.ShapeDtypeStruct((count, rows, rank), jnp.bfloat16),
        grid_spec=pltpu.PrefetchScalarGridSpec(
            num_scalar_prefetch=2,
            grid=(count // per_step,),
            in_specs=[pl.BlockSpec((held, tile, rank), lambda g, *_: (0, 0, 0))],
            out_specs=pl.BlockSpec((per_step, rows, rank), lambda g, *_: (g, 0, 0)),
        ),
        cost_estimate=pl.CostEstimate(
            flops=0, bytes_accessed=count * rows * rank * 2, transcendentals=0
        ),
        compiler_params=pltpu.CompilerParams(vmem_limit_bytes=VMEM_LIMIT),
    )(wanted, seg, item_blocks)


def tile_kernel(chunk, groups, user_ref, arrived_ref, feedback_ref, grad_ref, code_ref):
    @pl.when(pl.program_id(0) == 0)
    def _():
        grad_ref[...] = jnp.zeros_like(grad_ref)

    user = user_ref[...]
    users = user.shape[0]
    rows = arrived_ref.shape[1]
    tile = feedback_ref.shape[2]
    lane = lax.broadcasted_iota(jnp.int32, (users, tile), 1)
    residuals, blocks = [], []
    for pair in range(groups // 2):
        sides, items = [], []
        for half in range(2):
            first = (pair * 2 + half) * PARTS
            order = [first + (s - chunk) % PARTS for s in range(PARTS)]
            items += [arrived_ref[o] for o in order]
            seen = feedback_ref[order[PARTS - 1]].astype(jnp.float32)
            for s in range(PARTS - 2, -1, -1):
                seen = jnp.where(
                    lane < (s + 1) * rows, feedback_ref[order[s]].astype(jnp.float32), seen
                )
            sides.append(seen)
        block = jnp.concatenate(items, axis=0)
        scores = lax.dot_general(
            user, block, (((1,), (1,)), ((), ())), preferred_element_type=jnp.float32
        )
        residual = jnp.concatenate(
            [
                (jnp.tanh(scores[:, h * tile : (h + 1) * tile] * 0.5) * 0.5 + 0.5 - sides[h]).astype(
                    jnp.bfloat16
                )
                for h in range(2)
            ],
            axis=1,
        )
        part = lax.dot_general(
            residual, user, (((0,), (0,)), ((), ())), preferred_element_type=jnp.float32
        )
        code = encode(part)
        for half in range(2):
            first = (pair * 2 + half) * PARTS
            for s in range(PARTS):
                at = half * tile + s * rows
                code_ref[first + (s - chunk) % PARTS] = code[at : at + rows]
        residuals.append(residual)
        blocks.append(block)
    grad_ref[...] += jnp.dot(
        jnp.concatenate(residuals, axis=1),
        jnp.concatenate(blocks, axis=0),
        preferred_element_type=jnp.float32,
    )


def tiles(chunk, user_half, arrived, feedback):
    count, rows, rank = arrived.shape
    users = user_half.shape[0]
    tile = feedback.shape[2]
    per_step = 8
    work = count * rows * users * rank * 6
    return pl.pallas_call(
        functools.partial(tile_kernel, chunk, per_step // PARTS),
        out_shape=(
            jax.ShapeDtypeStruct((users, rank), jnp.float32),
            jax.ShapeDtypeStruct((count, rows, rank), jnp.int16),
        ),
        grid=(count // per_step,),
        in_specs=[
            pl.BlockSpec((users, rank), lambda g: (0, 0)),
            pl.BlockSpec((per_step, rows, rank), lambda g: (g, 0, 0)),
            pl.BlockSpec((per_step, users, tile), lambda g: (g, 0, 0)),
        ],
        out_specs=(
            pl.BlockSpec((users, rank), lambda g: (0, 0)),
            pl.BlockSpec((per_step, rows, rank), lambda g: (g, 0, 0)),
        ),
        cost_estimate=pl.CostEstimate(
            flops=work, bytes_accessed=count * users * tile * 2, transcendentals=0
        ),
        compiler_params=pltpu.CompilerParams(vmem_limit_bytes=VMEM_LIMIT),
    )(user_half, arrived, feedback)


def settle_kernel(
    per_step, last, wanted_ref, seg_ref, code_ref, item_ref, noise_ref, *refs
):
    if last:
        _, gathered_ref, user_ref, user_noise_ref, out_ref, new_user_ref, sum_ref = refs
        user = user_ref[...]
        total = gathered_ref[0]
        for z in range(1, gathered_ref.shape[0]):
            total = total + gathered_ref[z]
        new_user_ref[...] = (
            user - step_size * (total + prior_weight * user)
        ) + noise_scale * user_noise_ref[...]
    else:
        *_, out_ref, sum_ref = refs
    step = pl.program_id(0)

    @pl.when(step == 0)
    def _():
        sum_ref[...] = jnp.zeros_like(sum_ref)

    for j in range(per_step):
        block = wanted_ref[step * per_step + j]
        sum_ref[block] += decode(code_ref[j])

    @pl.when(step == pl.num_programs(0) - 1)
    def _():
        item = item_ref[...]
        out_ref[...] = (
            item - item_step * (sum_ref[...] + prior_weight * item)
        ) + item_noise_scale * noise_ref[...]


def settle(wanted, seg, codes, item_blocks, noise_blocks, before, user_side):
    count, rows, rank = codes.shape
    held = item_blocks.shape[0]
    per_step = 16
    steps = count // per_step
    part = pl.BlockSpec((held, rows, rank), lambda g, wanted_ref, seg_ref: (0, seg_ref[0], 0))
    in_specs = [pl.BlockSpec((per_step, rows, rank), lambda g, *_: (g, 0, 0)), part, part]
    out_specs = [part]
    out_shape = [jax.ShapeDtypeStruct(item_blocks.shape, jnp.float32)]
    operands = [wanted, seg, codes, item_blocks, noise_blocks]
    aliases = {}
    if before is not None:
        in_specs.append(pl.BlockSpec(memory_space=pl.ANY))
        aliases[len(operands)] = 0
        operands.append(before)
    if user_side is not None:
        users = user_side[1].shape[0]
        share = pl.BlockSpec((users // steps, rank), lambda g, *_: (g, 0))
        in_specs += [
            pl.BlockSpec((user_side[0].shape[0], users // steps, rank), lambda g, *_: (0, g, 0)),
            share,
            share,
        ]
        operands += user_side
        out_specs.append(share)
        out_shape.append(jax.ShapeDtypeStruct((users, rank), jnp.float32))
    return pl.pallas_call(
        functools.partial(settle_kernel, per_step, user_side is not None),
        out_shape=out_shape,
        grid_spec=pltpu.PrefetchScalarGridSpec(
            num_scalar_prefetch=2,
            grid=(steps,),
            in_specs=in_specs,
            out_specs=out_specs,
            scratch_shapes=[pltpu.VMEM((held, rows, rank), jnp.float32)],
        ),
        input_output_aliases=aliases,
        cost_estimate=pl.CostEstimate(
            flops=0, bytes_accessed=count * rows * rank * 8, transcendentals=0
        ),
        compiler_params=pltpu.CompilerParams(vmem_limit_bytes=VMEM_LIMIT),
    )(*operands)


def local(user_factors, item_factors, feedback, item_pick, user_noise, item_noise):
    own_index = lax.axis_index(AXES)
    tile_size = feedback.shape[2]
    rank_width = item_factors.shape[1]
    held_blocks = item_factors.shape[0] // tile_size
    rows = tile_size // PARTS
    wanted = lax.dynamic_slice_in_dim(item_pick, own_index, 1, 1)[:, 0]
    item_blocks = item_factors.reshape(held_blocks, tile_size, rank_width)
    noise_blocks = item_noise.reshape(held_blocks, tile_size, rank_width)
    user_half = user_factors.astype(jnp.bfloat16)
    segs = [((chunk + own_index) % PARTS).astype(jnp.int32)[None] for chunk in range(PARTS)]
    arrived = [
        lax.all_to_all(
            pack(item_blocks, wanted, seg, rows), AXES, split_axis=0, concat_axis=0, tiled=True
        )
        for seg in segs
    ]
    grads, returned = [], []
    for chunk in range(PARTS):
        grad, codes = tiles(chunk, user_half, arrived[chunk], feedback)
        grads.append(grad)
        returned.append(lax.all_to_all(codes, AXES, split_axis=0, concat_axis=0, tiled=True))
    gathered = lax.all_gather(functools.reduce(jnp.add, grads), "item")
    new_item = None
    for chunk in range(PARTS):
        user_side = [gathered, user_factors, user_noise] if chunk == PARTS - 1 else None
        new_item, *new_user = settle(
            wanted, segs[chunk], returned[chunk], item_blocks, noise_blocks, new_item, user_side
        )
    return (new_user[0], new_item.reshape(item_factors.shape))


def solution(mesh):
    in_specs = (
        P("user", None),
        P(("user", "item"), None),
        P("item", "user", None),
        P(),
        P("user", None),
        P(("user", "item"), None),
    )
    out_specs = (P("user", None), P(("user", "item"), None))
    return jax.shard_map(local, mesh=mesh, in_specs=in_specs, out_specs=out_specs, check_vma=False)
```

```python
import functools
import math

import jax
import jax.numpy as jnp
from jax import lax
from jax.experimental import pallas as pl
from jax.experimental.pallas import tpu as pltpu
from jax.sharding import Mesh
from jax.sharding import PartitionSpec as P

step_size = 0.01
item_step = 0.1
prior_weight = 1.0
noise_scale = math.sqrt(0.02)
item_noise_scale = math.sqrt(0.2)

VMEM_LIMIT = 63 * 1024 * 1024
SETTLE_COST = 1024
AXES = ("y", "x", "c", "z")
SIZES = (4, 4, 2, 4)

CODE_FLOOR = 2.0**-20
ITEM_RATE = 32700.0 / math.log(1.0 + 776.0 / CODE_FLOOR)
USER_RATE = 32700.0 / math.log(1.0 + 24800.0 / CODE_FLOOR)


def encode(part, rate):
    level = jnp.log(1.0 + jnp.abs(part) * (1.0 / CODE_FLOOR)) * rate + 0.5
    level = level.astype(jnp.int32)
    return jnp.where(part < 0.0, -level, level).astype(jnp.int16)


def decode(code, rate):
    code = code.astype(jnp.float32)
    size = jnp.exp(jnp.abs(code) * (1.0 / rate)) * CODE_FLOOR - CODE_FLOOR
    return jnp.where(code < 0.0, -size, size)


def place_of(own):
    return own // 32, own // 8 % 4, own // 4 % 2, own % 4


def call(kernel, scalars, operands, grid, in_specs, out_specs, out_shape, work, moved, scratch=(), aliases={}):
    return pl.pallas_call(
        kernel,
        out_shape=out_shape,
        grid_spec=pltpu.PrefetchScalarGridSpec(
            num_scalar_prefetch=len(scalars),
            grid=grid,
            in_specs=in_specs,
            out_specs=out_specs,
            scratch_shapes=scratch,
        ),
        input_output_aliases=aliases,
        cost_estimate=pl.CostEstimate(flops=work, bytes_accessed=moved, transcendentals=0),
        compiler_params=pltpu.CompilerParams(vmem_limit_bytes=VMEM_LIMIT),
    )(*scalars, *operands)


def whole(shape):
    return pl.BlockSpec(shape, lambda g, *_: (0,) * len(shape))


def along(shape):
    return pl.BlockSpec(shape, lambda g, *_: (g,) + (0,) * (len(shape) - 1))


ANY = pl.BlockSpec(memory_space=pl.ANY)


SEGMENTS = 4


def segments_of(p, first):
    return [(p + 1 + k) % SEGMENTS for k in range(SEGMENTS - 1)] if first else [p]


def row_slice(segment, rows):
    return pl.ds(pl.multiple_of(segment * rows, rows), rows)


def pack_kernel(first, own_ref, pick_ref, item_ref, out_ref, half_ref, sem):
    own = own_ref[0]
    count = out_ref.shape[0]
    rows = item_ref.shape[1] // SEGMENTS
    for k, segment in enumerate(segments_of(place_of(own)[3], first)):
        half_ref[:, k * rows : (k + 1) * rows, :] = item_ref[:, row_slice(segment, rows), :].astype(
            jnp.bfloat16
        )

    def send(e, _):
        pltpu.make_async_copy(half_ref.at[pick_ref[e, own]], out_ref.at[e], sem).start()
        return 0

    lax.fori_loop(0, count, send, 0, unroll=8)
    pltpu.make_async_copy(out_ref, out_ref, sem).wait()


def pack(first, own, item_pick, item_blocks):
    held, tile, rank = item_blocks.shape
    count = item_pick.shape[0]
    rows = tile // SEGMENTS * (SEGMENTS - 1 if first else 1)
    return call(
        functools.partial(pack_kernel, first),
        (own, item_pick),
        (item_blocks,),
        (1,),
        [whole(item_blocks.shape)],
        ANY,
        jax.ShapeDtypeStruct((count, rows, rank), jnp.bfloat16),
        0,
        count * rows * rank * 2,
        [pltpu.VMEM((held, rows, rank), jnp.bfloat16), pltpu.SemaphoreType.DMA],
    )


def work_on(first, user, arrived_ref, feedback_ref, code_ref):
    users, tile = feedback_ref.shape[1:]
    rows = tile // SEGMENTS
    lane = lax.broadcasted_iota(jnp.int32, (users, tile), 1)
    tiles = []
    for group in range(0, feedback_ref.shape[0], SEGMENTS):
        seen = [feedback_ref[group + p].astype(jnp.float32) for p in range(SEGMENTS)]
        for k in range(SEGMENTS - 1 if first else 1):
            sources = [(s - 1 - k) % SEGMENTS if first else s for s in range(SEGMENTS)]
            mixed = seen[sources[SEGMENTS - 1]]
            for s in range(SEGMENTS - 2, -1, -1):
                mixed = jnp.where(lane < (s + 1) * rows, seen[sources[s]], mixed)
            tiles.append((mixed, [group + p for p in sources], slice(k * rows, (k + 1) * rows)))
    residuals, blocks = [], []
    for pair in range(0, len(tiles), 2):
        both = tiles[pair : pair + 2]
        block = jnp.concatenate([arrived_ref[o, at] for _, owners, at in both for o in owners], axis=0)
        scores = lax.dot_general(
            user, block, (((1,), (1,)), ((), ())), preferred_element_type=jnp.float32
        )
        sides = []
        for h, (mixed, _, _) in enumerate(both):
            chance = jnp.tanh(scores[:, h * tile : (h + 1) * tile] * 0.5) * 0.5 + 0.5
            sides.append((chance - mixed).astype(jnp.bfloat16))
        residual = jnp.concatenate(sides, axis=1)
        part = lax.dot_general(
            residual, user, (((0,), (0,)), ((), ())), preferred_element_type=jnp.float32
        )
        code = encode(part, ITEM_RATE)
        for h, (_, owners, at) in enumerate(both):
            for s, o in enumerate(owners):
                code_ref[o, at] = code[h * tile + s * rows : h * tile + (s + 1) * rows]
        residuals.append(residual)
        blocks.append(block)
    return jnp.dot(
        jnp.concatenate(residuals, axis=1),
        jnp.concatenate(blocks, axis=0),
        preferred_element_type=jnp.float32,
    )


def first_kernel(user_ref, arrived_ref, feedback_ref, grad_ref, code_ref):
    @pl.when(pl.program_id(0) == 0)
    def _():
        grad_ref[...] = jnp.zeros_like(grad_ref)

    grad_ref[...] += work_on(True, user_ref[...], arrived_ref, feedback_ref, code_ref)


def last_kernel(user_ref, arrived_ref, feedback_ref, before_ref, grad_code_ref, code_ref, grad_ref):
    @pl.when(pl.program_id(0) == 0)
    def _():
        grad_ref[...] = before_ref[...]

    grad_ref[...] += work_on(False, user_ref[...], arrived_ref, feedback_ref, code_ref)

    @pl.when(pl.program_id(0) == pl.num_programs(0) - 1)
    def _():
        grad_code_ref[...] = encode(grad_ref[...], USER_RATE)


def tiles_of(user_half, arrived, feedback, before=None):
    count, rows, rank = arrived.shape
    users, tile = feedback.shape[1:]
    last = before is not None
    per_step = 16 if last else 8
    return call(
        last_kernel if last else first_kernel,
        (),
        (user_half, arrived, feedback) + ((before,) if last else ()),
        (count // per_step,),
        [whole((users, rank)), along((per_step, rows, rank)), along((per_step, users, tile))]
        + [whole((users, rank))] * last,
        [whole((users, rank)), along((per_step, rows, rank))],
        [
            jax.ShapeDtypeStruct((users, rank), jnp.int16 if last else jnp.float32),
            jax.ShapeDtypeStruct((count, rows, rank), jnp.int16),
        ],
        count * rows * users * rank * 6,
        count * users * tile * 2,
        [pltpu.VMEM((users, rank), jnp.float32)] * last,
    )


def add_codes(wanted_ref, code_ref, sum_ref):
    step = pl.program_id(0)

    @pl.when(step == 0)
    def _():
        sum_ref[...] = jnp.zeros_like(sum_ref)

    per_step = code_ref.shape[0]
    for j in range(per_step):
        sum_ref[wanted_ref[step * per_step + j]] += decode(code_ref[j], ITEM_RATE)


def stepped(item, grad, noise):
    return (item - item_step * (grad + prior_weight * item)) + item_noise_scale * noise


def first_settle_kernel(z_ref, wanted_ref, code_ref, item_ref, noise_ref, out_ref, sum_ref):
    add_codes(wanted_ref, code_ref, sum_ref)

    @pl.when(pl.program_id(0) == pl.num_programs(0) - 1)
    def _():
        rows = item_ref.shape[1] // SEGMENTS
        for k, segment in enumerate(segments_of(z_ref[0], True)):
            at = row_slice(segment, rows)
            grad = sum_ref[:, k * rows : (k + 1) * rows, :]
            out_ref[:, at, :] = stepped(item_ref[:, at, :], grad, noise_ref[:, at, :])


def first_settle(z, wanted, codes, item_blocks, noise_blocks):
    count, rows, rank = codes.shape
    per_step = 16
    block = whole(item_blocks.shape)
    return call(
        first_settle_kernel,
        (z, wanted),
        (codes, item_blocks, noise_blocks),
        (count // per_step,),
        [along((per_step, rows, rank)), block, block],
        block,
        jax.ShapeDtypeStruct(item_blocks.shape, jnp.float32),
        0,
        SETTLE_COST,
        [pltpu.VMEM((item_blocks.shape[0], rows, rank), jnp.float32)],
    )


def last_settle_kernel(z_ref, wanted_ref, code_ref, item_ref, noise_ref, before_ref, out_ref, sum_ref):
    add_codes(wanted_ref, code_ref, sum_ref)

    @pl.when(pl.program_id(0) == pl.num_programs(0) - 1)
    def _():
        out_ref[...] = stepped(item_ref[...], sum_ref[...], noise_ref[...])


def last_settle(z, wanted, codes, item_blocks, noise_blocks, before):
    count, rows, rank = codes.shape
    held = item_blocks.shape[0]
    per_step = 32
    part = pl.BlockSpec((held, rows, rank), lambda g, z_ref, wanted_ref: (0, z_ref[0], 0))
    return call(
        last_settle_kernel,
        (z, wanted),
        (codes, item_blocks, noise_blocks, before),
        (count // per_step,),
        [along((per_step, rows, rank)), part, part, ANY],
        part,
        jax.ShapeDtypeStruct(item_blocks.shape, jnp.float32),
        0,
        count * rows * rank * 8,
        [pltpu.VMEM((held, rows, rank), jnp.float32)],
        {5: 0},
    )


def user_kernel(z_ref, *refs):
    *code_refs, user_ref, noise_ref, out_ref, grads_ref = refs
    for j in range(4):
        grads_ref[(z_ref[0] + 4 - j) % 4] = decode(code_refs[j][...], USER_RATE)
    total = grads_ref[0] + grads_ref[1] + grads_ref[2] + grads_ref[3]
    user = user_ref[...]
    out_ref[...] = (user - step_size * (total + prior_weight * user)) + noise_scale * noise_ref[...]


def step_users(z, codes, user_factors, user_noise):
    users, rank = user_factors.shape
    steps = 4
    share = along((users // steps, rank))
    return call(
        user_kernel,
        (z,),
        (*codes, user_factors, user_noise),
        (steps,),
        [share] * 6,
        share,
        jax.ShapeDtypeStruct((users, rank), jnp.float32),
        0,
        users * rank * 16,
        [pltpu.VMEM((4, users // steps, rank), jnp.float32)],
    )


def shift(array, axis, j):
    return array if j == 0 else lax.ppermute(array, axis, [(i, (i + j) % 4) for i in range(4)])


def local(user_factors, item_factors, feedback, item_pick, user_noise, item_noise):
    own_index = lax.axis_index(AXES).astype(jnp.int32)
    own = own_index[None]
    z = lax.axis_index("z").astype(jnp.int32)[None]
    tile_size = feedback.shape[2]
    rank_width = item_factors.shape[1]
    held_blocks = item_factors.shape[0] // tile_size
    item_blocks = item_factors.reshape(held_blocks, tile_size, rank_width)
    noise_blocks = item_noise.reshape(held_blocks, tile_size, rank_width)
    user_half = user_factors.astype(jnp.bfloat16)
    to_all = functools.partial(
        lax.all_to_all, axis_name=AXES, split_axis=0, concat_axis=0, tiled=True
    )

    arrived = [to_all(pack(first, own, item_pick, item_blocks)) for first in (True, False)]
    picks, _ = lax.optimization_barrier((item_pick, arrived[0]))
    wanted = lax.dynamic_slice_in_dim(picks, own_index, 1, 1)[:, 0]
    grad, codes = tiles_of(user_half, arrived[0], feedback)
    returned = to_all(codes)
    grad_code, last_codes = tiles_of(user_half, arrived[1], feedback, grad)
    last_returned = to_all(last_codes)
    grad_codes = [shift(grad_code, "z", j) for j in range(4)]
    new_item = first_settle(z, wanted, returned, item_blocks, noise_blocks)
    new_item = last_settle(z, wanted, last_returned, item_blocks, noise_blocks, new_item)
    new_item, *grad_codes = lax.optimization_barrier((new_item, *grad_codes))
    new_user = step_users(z, grad_codes, user_factors, user_noise)
    return (new_user, new_item.reshape(item_factors.shape))


def solution(mesh):
    grid = Mesh(mesh.devices.reshape(SIZES), AXES)
    users, items = AXES[:3], AXES
    in_specs = (
        P(users, None),
        P(items, None),
        P("z", users, None),
        P(),
        P(users, None),
        P(items, None),
    )
    out_specs = (P(users, None), P(items, None))
    return jax.shard_map(local, mesh=grid, in_specs=in_specs, out_specs=out_specs, check_vma=False)
```

```python
import functools
import math

import jax
import jax.numpy as jnp
from jax import lax
from jax.experimental import pallas as pl
from jax.experimental.pallas import tpu as pltpu
from jax.sharding import Mesh
from jax.sharding import PartitionSpec as P

step_size = 0.01
item_step = 0.1
prior_weight = 1.0
noise_scale = math.sqrt(0.02)
item_noise_scale = math.sqrt(0.2)

VMEM_LIMIT = 63 * 1024 * 1024
SETTLE_COST = 1024
AXES = ("y", "x", "c", "z")
SIZES = (4, 4, 2, 4)

CODE_FLOOR = 2.0**-20
ITEM_RATE = 32700.0 / math.log(1.0 + 776.0 / CODE_FLOOR)
USER_RATE = 32700.0 / math.log(1.0 + 24800.0 / CODE_FLOOR)


def encode(part, rate):
    level = jnp.log(1.0 + jnp.abs(part) * (1.0 / CODE_FLOOR)) * rate + 0.5
    level = level.astype(jnp.int32)
    return jnp.where(part < 0.0, -level, level).astype(jnp.int16)


def decode(code, rate):
    code = code.astype(jnp.float32)
    size = jnp.exp(jnp.abs(code) * (1.0 / rate)) * CODE_FLOOR - CODE_FLOOR
    return jnp.where(code < 0.0, -size, size)


def place_of(own):
    return own // 32, own // 8 % 4, own // 4 % 2, own % 4


def call(kernel, scalars, operands, grid, in_specs, out_specs, out_shape, work, moved, scratch=(), aliases={}):
    return pl.pallas_call(
        kernel,
        out_shape=out_shape,
        grid_spec=pltpu.PrefetchScalarGridSpec(
            num_scalar_prefetch=len(scalars),
            grid=grid,
            in_specs=in_specs,
            out_specs=out_specs,
            scratch_shapes=scratch,
        ),
        input_output_aliases=aliases,
        cost_estimate=pl.CostEstimate(flops=work, bytes_accessed=moved, transcendentals=0),
        compiler_params=pltpu.CompilerParams(vmem_limit_bytes=VMEM_LIMIT),
    )(*scalars, *operands)


def whole(shape):
    return pl.BlockSpec(shape, lambda g, *_: (0,) * len(shape))


def along(shape):
    return pl.BlockSpec(shape, lambda g, *_: (g,) + (0,) * (len(shape) - 1))


ANY = pl.BlockSpec(memory_space=pl.ANY)


SEGMENTS = 4


def segments_of(p, first):
    return [(p + 1 + k) % SEGMENTS for k in range(SEGMENTS - 1)] if first else [p]


def row_slice(segment, rows):
    return pl.ds(pl.multiple_of(segment * rows, rows), rows)


def pack_kernel(first, own_ref, pick_ref, item_ref, out_ref, half_ref, sem):
    own = own_ref[0]
    count = out_ref.shape[0]
    rows = item_ref.shape[1] // SEGMENTS
    for k, segment in enumerate(segments_of(place_of(own)[3], first)):
        half_ref[:, k * rows : (k + 1) * rows, :] = item_ref[:, row_slice(segment, rows), :].astype(
            jnp.bfloat16
        )

    def send(e, _):
        pltpu.make_async_copy(half_ref.at[pick_ref[e, own]], out_ref.at[e], sem).start()
        return 0

    lax.fori_loop(0, count, send, 0, unroll=8)
    pltpu.make_async_copy(out_ref, out_ref, sem).wait()


def pack(first, own, item_pick, item_blocks):
    held, tile, rank = item_blocks.shape
    count = item_pick.shape[0]
    rows = tile // SEGMENTS * (SEGMENTS - 1 if first else 1)
    return call(
        functools.partial(pack_kernel, first),
        (own, item_pick),
        (item_blocks,),
        (1,),
        [whole(item_blocks.shape)],
        ANY,
        jax.ShapeDtypeStruct((count, rows, rank), jnp.bfloat16),
        0,
        count * rows * rank * 2,
        [pltpu.VMEM((held, rows, rank), jnp.bfloat16), pltpu.SemaphoreType.DMA],
    )


def work_on(first, user, arrived_ref, feedback_ref, code_ref):
    users, tile = feedback_ref.shape[1:]
    rows = tile // SEGMENTS
    lane = lax.broadcasted_iota(jnp.int32, (users, tile), 1)
    half_user = user * 0.5
    tiles = []
    for group in range(0, feedback_ref.shape[0], SEGMENTS):
        seen = [feedback_ref[group + p].astype(jnp.float32) for p in range(SEGMENTS)]
        for k in range(SEGMENTS - 1 if first else 1):
            sources = [(s - 1 - k) % SEGMENTS if first else s for s in range(SEGMENTS)]
            mixed = seen[sources[SEGMENTS - 1]]
            for s in range(SEGMENTS - 2, -1, -1):
                mixed = jnp.where(lane < (s + 1) * rows, seen[sources[s]], mixed)
            tiles.append((mixed, [group + p for p in sources], slice(k * rows, (k + 1) * rows)))
    residuals, blocks = [], []
    for pair in range(0, len(tiles), 2):
        both = tiles[pair : pair + 2]
        block = jnp.concatenate([arrived_ref[o, at] for _, owners, at in both for o in owners], axis=0)
        scores = lax.dot_general(
            half_user, block, (((1,), (1,)), ((), ())), preferred_element_type=jnp.float32
        )
        sides = []
        for h, (mixed, _, _) in enumerate(both):
            swing = jnp.tanh(scores[:, h * tile : (h + 1) * tile]) * 0.5
            sides.append((swing + (0.5 - mixed)).astype(jnp.bfloat16))
        residual = jnp.concatenate(sides, axis=1)
        part = lax.dot_general(
            residual, user, (((0,), (0,)), ((), ())), preferred_element_type=jnp.float32
        )
        code = encode(part, ITEM_RATE)
        for h, (_, owners, at) in enumerate(both):
            for s, o in enumerate(owners):
                code_ref[o, at] = code[h * tile + s * rows : h * tile + (s + 1) * rows]
        residuals.append(residual)
        blocks.append(block)
    return jnp.dot(
        jnp.concatenate(residuals, axis=1),
        jnp.concatenate(blocks, axis=0),
        preferred_element_type=jnp.float32,
    )


def first_kernel(user_ref, arrived_ref, feedback_ref, grad_ref, code_ref):
    @pl.when(pl.program_id(0) == 0)
    def _():
        grad_ref[...] = jnp.zeros_like(grad_ref)

    grad_ref[...] += work_on(True, user_ref[...], arrived_ref, feedback_ref, code_ref)


def last_kernel(
    user_ref,
    arrived_ref,
    feedback_ref,
    before_ref,
    factors_ref,
    noise_ref,
    grad_code_ref,
    code_ref,
    base_ref,
    grad_ref,
):
    @pl.when(pl.program_id(0) == 0)
    def _():
        grad_ref[...] = before_ref[...]

    grad_ref[...] += work_on(False, user_ref[...], arrived_ref, feedback_ref, code_ref)

    @pl.when(pl.program_id(0) == pl.num_programs(0) - 1)
    def _():
        grad_code_ref[...] = encode(grad_ref[...], USER_RATE)
        factors = factors_ref[...]
        base_ref[...] = (factors - step_size * prior_weight * factors) + noise_scale * noise_ref[...]


def tiles_of(user_half, arrived, feedback, *rest):
    count, rows, rank = arrived.shape
    users, tile = feedback.shape[1:]
    last = bool(rest)
    per_step = 16
    return call(
        last_kernel if last else first_kernel,
        (),
        (user_half, arrived, feedback, *rest),
        (count // per_step,),
        [whole((users, rank)), along((per_step, rows, rank)), along((per_step, users, tile))]
        + [whole((users, rank))] * len(rest),
        [whole((users, rank)), along((per_step, rows, rank))] + [whole((users, rank))] * last,
        [
            jax.ShapeDtypeStruct((users, rank), jnp.int16 if last else jnp.float32),
            jax.ShapeDtypeStruct((count, rows, rank), jnp.int16),
        ]
        + [jax.ShapeDtypeStruct((users, rank), jnp.float32)] * last,
        count * rows * users * rank * 6,
        count * users * tile * 2,
        [pltpu.VMEM((users, rank), jnp.float32)] * last,
    )


def add_codes(wanted_ref, code_ref, sum_ref):
    step = pl.program_id(0)

    @pl.when(step == 0)
    def _():
        sum_ref[...] = jnp.zeros_like(sum_ref)

    per_step = code_ref.shape[0]
    for j in range(per_step):
        sum_ref[wanted_ref[step * per_step + j]] += decode(code_ref[j], ITEM_RATE)


def stepped(item, grad, noise):
    return (item - item_step * (grad + prior_weight * item)) + item_noise_scale * noise


def first_settle_kernel(z_ref, wanted_ref, code_ref, item_ref, noise_ref, out_ref, sum_ref):
    add_codes(wanted_ref, code_ref, sum_ref)

    @pl.when(pl.program_id(0) == pl.num_programs(0) - 1)
    def _():
        rows = item_ref.shape[1] // SEGMENTS
        for k, segment in enumerate(segments_of(z_ref[0], True)):
            at = row_slice(segment, rows)
            grad = sum_ref[:, k * rows : (k + 1) * rows, :]
            out_ref[:, at, :] = stepped(item_ref[:, at, :], grad, noise_ref[:, at, :])


def first_settle(z, wanted, codes, item_blocks, noise_blocks):
    count, rows, rank = codes.shape
    per_step = 16
    block = whole(item_blocks.shape)
    return call(
        first_settle_kernel,
        (z, wanted),
        (codes, item_blocks, noise_blocks),
        (count // per_step,),
        [along((per_step, rows, rank)), block, block],
        block,
        jax.ShapeDtypeStruct(item_blocks.shape, jnp.float32),
        0,
        SETTLE_COST,
        [pltpu.VMEM((item_blocks.shape[0], rows, rank), jnp.float32)],
    )


def last_settle_kernel(
    z_ref, wanted_ref, code_ref, item_ref, noise_ref, before_ref, out_ref, done_ref, sum_ref
):
    add_codes(wanted_ref, code_ref, sum_ref)

    @pl.when(pl.program_id(0) == pl.num_programs(0) - 1)
    def _():
        out_ref[...] = stepped(item_ref[...], sum_ref[...], noise_ref[...])
        done_ref[...] = jnp.zeros_like(done_ref)


def last_settle(z, wanted, codes, item_blocks, noise_blocks, before):
    count, rows, rank = codes.shape
    held = item_blocks.shape[0]
    per_step = 64
    part = pl.BlockSpec((held, rows, rank), lambda g, z_ref, wanted_ref: (0, z_ref[0], 0))
    return call(
        last_settle_kernel,
        (z, wanted),
        (codes, item_blocks, noise_blocks, before),
        (count // per_step,),
        [along((per_step, rows, rank)), part, part, ANY],
        [part, whole((8, 128))],
        [
            jax.ShapeDtypeStruct(item_blocks.shape, jnp.float32),
            jax.ShapeDtypeStruct((8, 128), jnp.float32),
        ],
        0,
        count * rows * rank * 8,
        [pltpu.VMEM((held, rows, rank), jnp.float32)],
        {5: 0},
    )


def user_kernel(z_ref, *refs):
    *code_refs, base_ref, _, out_ref, grads_ref = refs
    z = z_ref[0]
    rows = grads_ref.shape[1]

    def piece(i, _):
        at = row_slice(i, rows)
        for j in range(4):
            grads_ref[(z + 4 - j) % 4] = decode(code_refs[j][at, :], USER_RATE)
        total = grads_ref[0] + grads_ref[1] + grads_ref[2] + grads_ref[3]
        out_ref[at, :] = base_ref[at, :] - step_size * total
        return 0

    lax.fori_loop(0, base_ref.shape[0] // rows, piece, 0, unroll=2)


def step_users(z, codes, base, after):
    users, rank = base.shape
    steps = 2
    share = along((users // steps, rank))
    return pl.pallas_call(
        user_kernel,
        out_shape=jax.ShapeDtypeStruct((users, rank), jnp.float32),
        grid_spec=pltpu.PrefetchScalarGridSpec(
            num_scalar_prefetch=1,
            grid=(steps,),
            in_specs=[share] * 5 + [whole(after.shape)],
            out_specs=share,
            scratch_shapes=[pltpu.VMEM((4, 32, rank), jnp.float32)],
        ),
        cost_estimate=pl.CostEstimate(flops=0, bytes_accessed=users * rank * 16, transcendentals=0),
        compiler_params=pltpu.CompilerParams(vmem_limit_bytes=16 * 1024 * 1024),
    )(z, *codes, base, after)


def shift(array, axis, j):
    return array if j == 0 else lax.ppermute(array, axis, [(i, (i + j) % 4) for i in range(4)])


def local(user_factors, item_factors, feedback, item_pick, user_noise, item_noise):
    own_index = lax.axis_index(AXES).astype(jnp.int32)
    own = own_index[None]
    z = lax.axis_index("z").astype(jnp.int32)[None]
    tile_size = feedback.shape[2]
    rank_width = item_factors.shape[1]
    held_blocks = item_factors.shape[0] // tile_size
    item_blocks = item_factors.reshape(held_blocks, tile_size, rank_width)
    noise_blocks = item_noise.reshape(held_blocks, tile_size, rank_width)
    user_half = user_factors.astype(jnp.bfloat16)
    to_all = functools.partial(
        lax.all_to_all, axis_name=AXES, split_axis=0, concat_axis=0, tiled=True
    )

    arrived = [to_all(pack(first, own, item_pick, item_blocks)) for first in (True, False)]
    picks, _ = lax.optimization_barrier((item_pick, arrived[0]))
    wanted = lax.dynamic_slice_in_dim(picks, own_index, 1, 1)[:, 0]
    grad, codes = tiles_of(user_half, arrived[0], feedback)
    returned = to_all(codes)
    grad_code, last_codes, base = tiles_of(
        user_half, arrived[1], feedback, grad, user_factors, user_noise
    )
    last_returned = to_all(last_codes)
    grad_codes = [shift(grad_code, "z", j) for j in range(4)]
    new_item = first_settle(z, wanted, returned, item_blocks, noise_blocks)
    new_item, done = last_settle(z, wanted, last_returned, item_blocks, noise_blocks, new_item)
    new_user = step_users(z, grad_codes, base, done)
    return (new_user, new_item.reshape(item_factors.shape))


def solution(mesh):
    grid = Mesh(mesh.devices.reshape(SIZES), AXES)
    users, items = AXES[:3], AXES
    in_specs = (
        P(users, None),
        P(items, None),
        P("z", users, None),
        P(),
        P(users, None),
        P(items, None),
    )
    out_specs = (P(users, None), P(items, None))
    return jax.shard_map(local, mesh=grid, in_specs=in_specs, out_specs=out_specs, check_vma=False)
```

```python
import functools
import math

import jax
import jax.numpy as jnp
from jax import lax
from jax.experimental import pallas as pl
from jax.experimental.pallas import tpu as pltpu
from jax.sharding import Mesh
from jax.sharding import PartitionSpec as P

step_size = 0.01
item_step = 0.1
prior_weight = 1.0
noise_scale = math.sqrt(0.02)
item_noise_scale = math.sqrt(0.2)

VMEM_LIMIT = 63 * 1024 * 1024
SETTLE_COST = 1024
AXES = ("y", "x", "c", "z")
SIZES = (4, 4, 2, 4)

CODE_FLOOR = 2.0**-20
ITEM_RATE = 32700.0 / math.log(1.0 + 776.0 / CODE_FLOOR)
USER_RATE = 32700.0 / math.log(1.0 + 24800.0 / CODE_FLOOR)


def encode(part, rate):
    level = jnp.log(1.0 + jnp.abs(part) * (1.0 / CODE_FLOOR)) * rate + 0.5
    level = level.astype(jnp.int32)
    return jnp.where(part < 0.0, -level, level).astype(jnp.int16)


def decode(code, rate):
    code = code.astype(jnp.float32)
    size = jnp.exp(jnp.abs(code) * (1.0 / rate)) * CODE_FLOOR - CODE_FLOOR
    return jnp.where(code < 0.0, -size, size)


def place_of(own):
    return own // 32, own // 8 % 4, own // 4 % 2, own % 4


def call(kernel, scalars, operands, grid, in_specs, out_specs, out_shape, work, moved, scratch=(), aliases={}):
    return pl.pallas_call(
        kernel,
        out_shape=out_shape,
        grid_spec=pltpu.PrefetchScalarGridSpec(
            num_scalar_prefetch=len(scalars),
            grid=grid,
            in_specs=in_specs,
            out_specs=out_specs,
            scratch_shapes=scratch,
        ),
        input_output_aliases=aliases,
        cost_estimate=pl.CostEstimate(flops=work, bytes_accessed=moved, transcendentals=0),
        compiler_params=pltpu.CompilerParams(vmem_limit_bytes=VMEM_LIMIT),
    )(*scalars, *operands)


def whole(shape):
    return pl.BlockSpec(shape, lambda g, *_: (0,) * len(shape))


def along(shape):
    return pl.BlockSpec(shape, lambda g, *_: (g,) + (0,) * (len(shape) - 1))


ANY = pl.BlockSpec(memory_space=pl.ANY)


SEGMENTS = 2


def segments_of(p, first):
    return [(p + 1 + k) % SEGMENTS for k in range(SEGMENTS - 1)] if first else [p % SEGMENTS]


def row_slice(segment, rows):
    return pl.ds(pl.multiple_of(segment * rows, rows), rows)


def pack_kernel(first, own_ref, pick_ref, item_ref, out_ref, half_ref, sem):
    own = own_ref[0]
    count = out_ref.shape[0]
    rows = item_ref.shape[1] // SEGMENTS
    for k, segment in enumerate(segments_of(place_of(own)[3], first)):
        half_ref[:, k * rows : (k + 1) * rows, :] = item_ref[:, row_slice(segment, rows), :].astype(
            jnp.bfloat16
        )

    def send(e, _):
        pltpu.make_async_copy(half_ref.at[pick_ref[e, own]], out_ref.at[e], sem).start()
        return 0

    lax.fori_loop(0, count, send, 0, unroll=8)
    pltpu.make_async_copy(out_ref, out_ref, sem).wait()


def pack(first, own, item_pick, item_blocks):
    held, tile, rank = item_blocks.shape
    count = item_pick.shape[0]
    rows = tile // SEGMENTS * (SEGMENTS - 1 if first else 1)
    return call(
        functools.partial(pack_kernel, first),
        (own,),
        (item_pick, item_blocks),
        (1,),
        [pl.BlockSpec(memory_space=pltpu.SMEM), whole(item_blocks.shape)],
        ANY,
        jax.ShapeDtypeStruct((count, rows, rank), jnp.bfloat16),
        0,
        count * rows * rank * 2,
        [pltpu.VMEM((held, rows, rank), jnp.bfloat16), pltpu.SemaphoreType.DMA],
    )


def work_on(first, user, arrived_ref, feedback_ref, code_ref):
    users, tile = feedback_ref.shape[1:]
    rows = tile // SEGMENTS
    lane = lax.broadcasted_iota(jnp.int32, (users, tile), 1)
    half_user = user * 0.5
    tiles = []
    for group in range(0, feedback_ref.shape[0], SEGMENTS):
        seen = [feedback_ref[group + p].astype(jnp.float32) for p in range(SEGMENTS)]
        for k in range(SEGMENTS - 1 if first else 1):
            sources = [(s - 1 - k) % SEGMENTS if first else s for s in range(SEGMENTS)]
            mixed = seen[sources[SEGMENTS - 1]]
            for s in range(SEGMENTS - 2, -1, -1):
                mixed = jnp.where(lane < (s + 1) * rows, seen[sources[s]], mixed)
            tiles.append((mixed, [group + p for p in sources], slice(k * rows, (k + 1) * rows)))
    residuals, blocks = [], []
    for pair in range(0, len(tiles), 2):
        both = tiles[pair : pair + 2]
        block = jnp.concatenate([arrived_ref[o, at] for _, owners, at in both for o in owners], axis=0)
        scores = lax.dot_general(
            half_user, block, (((1,), (1,)), ((), ())), preferred_element_type=jnp.float32
        )
        sides = []
        for h, (mixed, _, _) in enumerate(both):
            swing = jnp.tanh(scores[:, h * tile : (h + 1) * tile]) * 0.5
            sides.append((swing + (0.5 - mixed)).astype(jnp.bfloat16))
        residual = jnp.concatenate(sides, axis=1)
        part = lax.dot_general(
            residual, user, (((0,), (0,)), ((), ())), preferred_element_type=jnp.float32
        )
        code = encode(part, ITEM_RATE)
        for h, (_, owners, at) in enumerate(both):
            for s, o in enumerate(owners):
                code_ref[o, at] = code[h * tile + s * rows : h * tile + (s + 1) * rows]
        residuals.append(residual)
        blocks.append(block)
    return jnp.dot(
        jnp.concatenate(residuals, axis=1),
        jnp.concatenate(blocks, axis=0),
        preferred_element_type=jnp.float32,
    )


def first_kernel(user_ref, arrived_ref, feedback_ref, grad_ref, code_ref):
    @pl.when(pl.program_id(0) == 0)
    def _():
        grad_ref[...] = jnp.zeros_like(grad_ref)

    grad_ref[...] += work_on(True, user_ref[...], arrived_ref, feedback_ref, code_ref)


def last_kernel(
    user_ref,
    arrived_ref,
    feedback_ref,
    before_ref,
    factors_ref,
    noise_ref,
    grad_code_ref,
    code_ref,
    base_ref,
    grad_ref,
):
    @pl.when(pl.program_id(0) == 0)
    def _():
        grad_ref[...] = before_ref[...]

    grad_ref[...] += work_on(False, user_ref[...], arrived_ref, feedback_ref, code_ref)

    @pl.when(pl.program_id(0) == pl.num_programs(0) - 1)
    def _():
        grad_code_ref[...] = encode(grad_ref[...], USER_RATE)
        factors = factors_ref[...]
        base_ref[...] = (factors - step_size * prior_weight * factors) + noise_scale * noise_ref[...]


def tiles_of(user_half, arrived, feedback, *rest):
    count, rows, rank = arrived.shape
    users, tile = feedback.shape[1:]
    last = bool(rest)
    per_step = 16
    return call(
        last_kernel if last else first_kernel,
        (),
        (user_half, arrived, feedback, *rest),
        (count // per_step,),
        [whole((users, rank)), along((per_step, rows, rank)), along((per_step, users, tile))]
        + [whole((users, rank))] * len(rest),
        [whole((users, rank)), along((per_step, rows, rank))] + [whole((users, rank))] * last,
        [
            jax.ShapeDtypeStruct((users, rank), jnp.int16 if last else jnp.float32),
            jax.ShapeDtypeStruct((count, rows, rank), jnp.int16),
        ]
        + [jax.ShapeDtypeStruct((users, rank), jnp.float32)] * last,
        count * rows * users * rank * 6,
        count * users * tile * 2,
        [pltpu.VMEM((users, rank), jnp.float32)] * last,
    )


def add_codes(wanted_ref, code_ref, sum_ref):
    step = pl.program_id(0)

    @pl.when(step == 0)
    def _():
        sum_ref[...] = jnp.zeros_like(sum_ref)

    per_step = code_ref.shape[0]
    for j in range(per_step):
        sum_ref[wanted_ref[step * per_step + j]] += decode(code_ref[j], ITEM_RATE)


def stepped(item, grad, noise):
    return (item - item_step * (grad + prior_weight * item)) + item_noise_scale * noise


def first_settle_kernel(z_ref, wanted_ref, code_ref, item_ref, noise_ref, out_ref, sum_ref):
    add_codes(wanted_ref, code_ref, sum_ref)

    @pl.when(pl.program_id(0) == pl.num_programs(0) - 1)
    def _():
        rows = item_ref.shape[1] // SEGMENTS
        for k, segment in enumerate(segments_of(z_ref[0], True)):
            at = row_slice(segment, rows)
            grad = sum_ref[:, k * rows : (k + 1) * rows, :]
            out_ref[:, at, :] = stepped(item_ref[:, at, :], grad, noise_ref[:, at, :])


def first_settle(z, wanted, codes, item_blocks, noise_blocks):
    count, rows, rank = codes.shape
    per_step = 16
    block = whole(item_blocks.shape)
    return call(
        first_settle_kernel,
        (z, wanted),
        (codes, item_blocks, noise_blocks),
        (count // per_step,),
        [along((per_step, rows, rank)), block, block],
        block,
        jax.ShapeDtypeStruct(item_blocks.shape, jnp.float32),
        0,
        SETTLE_COST,
        [pltpu.VMEM((item_blocks.shape[0], rows, rank), jnp.float32)],
    )


def last_settle_kernel(
    z_ref, wanted_ref, code_ref, item_ref, noise_ref, before_ref, out_ref, done_ref, sum_ref
):
    add_codes(wanted_ref, code_ref, sum_ref)

    @pl.when(pl.program_id(0) == pl.num_programs(0) - 1)
    def _():
        out_ref[...] = stepped(item_ref[...], sum_ref[...], noise_ref[...])
        done_ref[...] = jnp.zeros_like(done_ref)


def last_settle(z, wanted, codes, item_blocks, noise_blocks, before):
    count, rows, rank = codes.shape
    held = item_blocks.shape[0]
    per_step = 64
    part = pl.BlockSpec((held, rows, rank), lambda g, z_ref, wanted_ref: (0, z_ref[0], 0))
    return call(
        last_settle_kernel,
        (z, wanted),
        (codes, item_blocks, noise_blocks, before),
        (count // per_step,),
        [along((per_step, rows, rank)), part, part, ANY],
        [part, whole((8, 128))],
        [
            jax.ShapeDtypeStruct(item_blocks.shape, jnp.float32),
            jax.ShapeDtypeStruct((8, 128), jnp.float32),
        ],
        0,
        count * rows * rank * 8,
        [pltpu.VMEM((held, rows, rank), jnp.float32)],
        {5: 0},
    )


def user_kernel(z_ref, *refs):
    *code_refs, base_ref, _, out_ref, grads_ref = refs
    z = z_ref[0]
    rows = grads_ref.shape[1]

    def piece(i, _):
        at = row_slice(i, rows)
        for j in range(4):
            grads_ref[(z + 4 - j) % 4] = decode(code_refs[j][at, :], USER_RATE)
        total = grads_ref[0] + grads_ref[1] + grads_ref[2] + grads_ref[3]
        out_ref[at, :] = base_ref[at, :] - step_size * total
        return 0

    lax.fori_loop(0, base_ref.shape[0] // rows, piece, 0, unroll=2)


def step_users(z, codes, base, after):
    users, rank = base.shape
    steps = 2
    share = along((users // steps, rank))
    return pl.pallas_call(
        user_kernel,
        out_shape=jax.ShapeDtypeStruct((users, rank), jnp.float32),
        grid_spec=pltpu.PrefetchScalarGridSpec(
            num_scalar_prefetch=1,
            grid=(steps,),
            in_specs=[share] * 5 + [whole(after.shape)],
            out_specs=share,
            scratch_shapes=[pltpu.VMEM((4, 32, rank), jnp.float32)],
        ),
        cost_estimate=pl.CostEstimate(flops=0, bytes_accessed=users * rank * 16, transcendentals=0),
        compiler_params=pltpu.CompilerParams(vmem_limit_bytes=16 * 1024 * 1024),
    )(z, *codes, base, after)


def shift(array, axis, j):
    return array if j == 0 else lax.ppermute(array, axis, [(i, (i + j) % 4) for i in range(4)])


def local(user_factors, item_factors, feedback, item_pick, user_noise, item_noise):
    own_index = lax.axis_index(AXES).astype(jnp.int32)
    own = own_index[None]
    z = lax.axis_index("z").astype(jnp.int32)[None]
    tile_size = feedback.shape[2]
    rank_width = item_factors.shape[1]
    held_blocks = item_factors.shape[0] // tile_size
    item_blocks = item_factors.reshape(held_blocks, tile_size, rank_width)
    noise_blocks = item_noise.reshape(held_blocks, tile_size, rank_width)
    user_half = user_factors.astype(jnp.bfloat16)
    to_all = functools.partial(
        lax.all_to_all, axis_name=AXES, split_axis=0, concat_axis=0, tiled=True
    )

    arrived = [to_all(pack(first, own, item_pick, item_blocks)) for first in (True, False)]
    picks, _ = lax.optimization_barrier((item_pick, arrived[0]))
    wanted = lax.dynamic_slice_in_dim(picks, own_index, 1, 1)[:, 0]
    grad, codes = tiles_of(user_half, arrived[0], feedback)
    returned = to_all(codes)
    grad_code, last_codes, base = tiles_of(
        user_half, arrived[1], feedback, grad, user_factors, user_noise
    )
    last_returned = to_all(last_codes)
    grad_codes = [shift(grad_code, "z", j) for j in range(4)]
    new_item = first_settle(z % SEGMENTS, wanted, returned, item_blocks, noise_blocks)
    new_item, done = last_settle(z % SEGMENTS, wanted, last_returned, item_blocks, noise_blocks, new_item)
    new_user = step_users(z, grad_codes, base, done)
    return (new_user, new_item.reshape(item_factors.shape))


def solution(mesh):
    grid = Mesh(mesh.devices.reshape(SIZES), AXES)
    users, items = AXES[:3], AXES
    in_specs = (
        P(users, None),
        P(items, None),
        P("z", users, None),
        P(),
        P(users, None),
        P(items, None),
    )
    out_specs = (P(users, None), P(items, None))
    return jax.shard_map(local, mesh=grid, in_specs=in_specs, out_specs=out_specs, check_vma=False)
```

```python
import functools
import math

import jax
import jax.numpy as jnp
from jax import lax
from jax.experimental import pallas as pl
from jax.experimental.pallas import tpu as pltpu
from jax.sharding import Mesh
from jax.sharding import PartitionSpec as P

step_size = 0.01
item_step = 0.1
prior_weight = 1.0
noise_scale = math.sqrt(0.02)
item_noise_scale = math.sqrt(0.2)

VMEM_LIMIT = 63 * 1024 * 1024
SETTLE_COST = 1024
AXES = ("y", "x", "c", "z")
SIZES = (4, 4, 2, 4)

CODE_FLOOR = 2.0**-20
ITEM_RATE = 32700.0 / math.log(1.0 + 776.0 / CODE_FLOOR)
USER_RATE = 32700.0 / math.log(1.0 + 24800.0 / CODE_FLOOR)


def encode(part, rate):
    level = jnp.log(1.0 + jnp.abs(part) * (1.0 / CODE_FLOOR)) * rate + 0.5
    level = level.astype(jnp.int32)
    return jnp.where(part < 0.0, -level, level).astype(jnp.int16)


def decode(code, rate):
    code = code.astype(jnp.float32)
    size = jnp.exp(jnp.abs(code) * (1.0 / rate)) - 1.0
    return jnp.where(code < 0.0, -size, size)


def place_of(own):
    return own // 32, own // 8 % 4, own // 4 % 2, own % 4


def call(kernel, scalars, operands, grid, in_specs, out_specs, out_shape, work, moved, scratch=(), aliases={}):
    return pl.pallas_call(
        kernel,
        out_shape=out_shape,
        grid_spec=pltpu.PrefetchScalarGridSpec(
            num_scalar_prefetch=len(scalars),
            grid=grid,
            in_specs=in_specs,
            out_specs=out_specs,
            scratch_shapes=scratch,
        ),
        input_output_aliases=aliases,
        cost_estimate=pl.CostEstimate(flops=work, bytes_accessed=moved, transcendentals=0),
        compiler_params=pltpu.CompilerParams(vmem_limit_bytes=VMEM_LIMIT),
    )(*scalars, *operands)


def whole(shape):
    return pl.BlockSpec(shape, lambda g, *_: (0,) * len(shape))


def along(shape):
    return pl.BlockSpec(shape, lambda g, *_: (g,) + (0,) * (len(shape) - 1))


ANY = pl.BlockSpec(memory_space=pl.ANY)


SEGMENTS = 2


def segments_of(p, first):
    return [(p + 1 + k) % SEGMENTS for k in range(SEGMENTS - 1)] if first else [p % SEGMENTS]


def row_slice(segment, rows):
    return pl.ds(pl.multiple_of(segment * rows, rows), rows)


def pack_kernel(first, own_ref, pick_ref, item_ref, out_ref, half_ref, sem):
    own = own_ref[0]
    count = out_ref.shape[0]
    rows = item_ref.shape[1] // SEGMENTS
    for k, segment in enumerate(segments_of(place_of(own)[3], first)):
        half_ref[:, k * rows : (k + 1) * rows, :] = item_ref[:, row_slice(segment, rows), :].astype(
            jnp.bfloat16
        )

    def send(e, _):
        pltpu.make_async_copy(half_ref.at[pick_ref[e, own]], out_ref.at[e], sem).start()
        return 0

    lax.fori_loop(0, count, send, 0, unroll=8)
    pltpu.make_async_copy(out_ref, out_ref, sem).wait()


def pack(first, own, item_pick, item_blocks):
    held, tile, rank = item_blocks.shape
    count = item_pick.shape[0]
    rows = tile // SEGMENTS * (SEGMENTS - 1 if first else 1)
    return call(
        functools.partial(pack_kernel, first),
        (own,),
        (item_pick, item_blocks),
        (1,),
        [pl.BlockSpec(memory_space=pltpu.SMEM), whole(item_blocks.shape)],
        ANY,
        jax.ShapeDtypeStruct((count, rows, rank), jnp.bfloat16),
        0,
        count * rows * rank * 2,
        [pltpu.VMEM((held, rows, rank), jnp.bfloat16), pltpu.SemaphoreType.DMA],
    )


def work_on(first, user, arrived_ref, feedback_ref, code_ref):
    users, tile = feedback_ref.shape[1:]
    rows = tile // SEGMENTS
    lane = lax.broadcasted_iota(jnp.int32, (users, tile), 1)
    half_user = user * 0.5
    tiles = []
    for group in range(0, feedback_ref.shape[0], SEGMENTS):
        seen = [feedback_ref[group + p].astype(jnp.float32) for p in range(SEGMENTS)]
        for k in range(SEGMENTS - 1 if first else 1):
            sources = [(s - 1 - k) % SEGMENTS if first else s for s in range(SEGMENTS)]
            mixed = seen[sources[SEGMENTS - 1]]
            for s in range(SEGMENTS - 2, -1, -1):
                mixed = jnp.where(lane < (s + 1) * rows, seen[sources[s]], mixed)
            tiles.append((mixed, [group + p for p in sources], slice(k * rows, (k + 1) * rows)))
    residuals, blocks = [], []
    for pair in range(0, len(tiles), 2):
        both = tiles[pair : pair + 2]
        block = jnp.concatenate([arrived_ref[o, at] for _, owners, at in both for o in owners], axis=0)
        scores = lax.dot_general(
            half_user, block, (((1,), (1,)), ((), ())), preferred_element_type=jnp.float32
        )
        sides = []
        for h, (mixed, _, _) in enumerate(both):
            swing = jnp.tanh(scores[:, h * tile : (h + 1) * tile]) * 0.5
            sides.append((swing + (0.5 - mixed)).astype(jnp.bfloat16))
        residual = jnp.concatenate(sides, axis=1)
        part = lax.dot_general(
            residual, user, (((0,), (0,)), ((), ())), preferred_element_type=jnp.float32
        )
        code = encode(part, ITEM_RATE)
        for h, (_, owners, at) in enumerate(both):
            for s, o in enumerate(owners):
                code_ref[o, at] = code[h * tile + s * rows : h * tile + (s + 1) * rows]
        residuals.append(residual)
        blocks.append(block)
    return jnp.dot(
        jnp.concatenate(residuals, axis=1),
        jnp.concatenate(blocks, axis=0),
        preferred_element_type=jnp.float32,
    )


def first_kernel(user_ref, arrived_ref, feedback_ref, grad_ref, code_ref):
    @pl.when(pl.program_id(0) == 0)
    def _():
        grad_ref[...] = jnp.zeros_like(grad_ref)

    grad_ref[...] += work_on(True, user_ref[...], arrived_ref, feedback_ref, code_ref)


def last_kernel(
    user_ref,
    arrived_ref,
    feedback_ref,
    before_ref,
    factors_ref,
    noise_ref,
    grad_code_ref,
    code_ref,
    base_ref,
    grad_ref,
):
    @pl.when(pl.program_id(0) == 0)
    def _():
        grad_ref[...] = before_ref[...]

    grad_ref[...] += work_on(False, user_ref[...], arrived_ref, feedback_ref, code_ref)

    @pl.when(pl.program_id(0) == pl.num_programs(0) - 1)
    def _():
        grad_code_ref[...] = encode(grad_ref[...], USER_RATE)
        factors = factors_ref[...]
        base_ref[...] = (factors - step_size * prior_weight * factors) + noise_scale * noise_ref[...]


def tiles_of(user_half, arrived, feedback, *rest):
    count, rows, rank = arrived.shape
    users, tile = feedback.shape[1:]
    last = bool(rest)
    per_step = 16
    return call(
        last_kernel if last else first_kernel,
        (),
        (user_half, arrived, feedback, *rest),
        (count // per_step,),
        [whole((users, rank)), along((per_step, rows, rank)), along((per_step, users, tile))]
        + [whole((users, rank))] * len(rest),
        [whole((users, rank)), along((per_step, rows, rank))] + [whole((users, rank))] * last,
        [
            jax.ShapeDtypeStruct((users, rank), jnp.int16 if last else jnp.float32),
            jax.ShapeDtypeStruct((count, rows, rank), jnp.int16),
        ]
        + [jax.ShapeDtypeStruct((users, rank), jnp.float32)] * last,
        count * rows * users * rank * 6,
        count * users * tile * 2,
        [pltpu.VMEM((users, rank), jnp.float32)] * last,
    )


def add_codes(wanted_ref, code_ref, sum_ref):
    step = pl.program_id(0)

    @pl.when(step == 0)
    def _():
        sum_ref[...] = jnp.zeros_like(sum_ref)

    per_step = code_ref.shape[0]
    for j in range(per_step):
        sum_ref[wanted_ref[step * per_step + j]] += decode(code_ref[j], ITEM_RATE)


def stepped(item, grad, noise):
    return (item - item_step * (grad * CODE_FLOOR + prior_weight * item)) + item_noise_scale * noise


def first_settle_kernel(z_ref, wanted_ref, code_ref, item_ref, noise_ref, out_ref, sum_ref):
    add_codes(wanted_ref, code_ref, sum_ref)

    @pl.when(pl.program_id(0) == pl.num_programs(0) - 1)
    def _():
        rows = item_ref.shape[1] // SEGMENTS
        for k, segment in enumerate(segments_of(z_ref[0], True)):
            at = row_slice(segment, rows)
            grad = sum_ref[:, k * rows : (k + 1) * rows, :]
            out_ref[:, at, :] = stepped(item_ref[:, at, :], grad, noise_ref[:, at, :])


def first_settle(z, wanted, codes, item_blocks, noise_blocks):
    count, rows, rank = codes.shape
    per_step = 32
    block = whole(item_blocks.shape)
    return call(
        first_settle_kernel,
        (z, wanted),
        (codes, item_blocks, noise_blocks),
        (count // per_step,),
        [along((per_step, rows, rank)), block, block],
        block,
        jax.ShapeDtypeStruct(item_blocks.shape, jnp.float32),
        0,
        SETTLE_COST,
        [pltpu.VMEM((item_blocks.shape[0], rows, rank), jnp.float32)],
    )


def last_settle_kernel(
    z_ref, wanted_ref, code_ref, item_ref, noise_ref, before_ref, out_ref, done_ref, sum_ref
):
    add_codes(wanted_ref, code_ref, sum_ref)

    @pl.when(pl.program_id(0) == pl.num_programs(0) - 1)
    def _():
        out_ref[...] = stepped(item_ref[...], sum_ref[...], noise_ref[...])
        done_ref[...] = jnp.zeros_like(done_ref)


def last_settle(z, wanted, codes, item_blocks, noise_blocks, before):
    count, rows, rank = codes.shape
    held = item_blocks.shape[0]
    per_step = 64
    part = pl.BlockSpec((held, rows, rank), lambda g, z_ref, wanted_ref: (0, z_ref[0], 0))
    return call(
        last_settle_kernel,
        (z, wanted),
        (codes, item_blocks, noise_blocks, before),
        (count // per_step,),
        [along((per_step, rows, rank)), part, part, ANY],
        [part, whole((8, 128))],
        [
            jax.ShapeDtypeStruct(item_blocks.shape, jnp.float32),
            jax.ShapeDtypeStruct((8, 128), jnp.float32),
        ],
        0,
        count * rows * rank * 8,
        [pltpu.VMEM((held, rows, rank), jnp.float32)],
        {5: 0},
    )


def user_kernel(z_ref, *refs):
    *code_refs, base_ref, _, out_ref, grads_ref = refs
    z = z_ref[0]
    rows = grads_ref.shape[1]

    def piece(i, _):
        at = row_slice(i, rows)
        for j in range(4):
            grads_ref[(z + 4 - j) % 4] = decode(code_refs[j][at, :], USER_RATE)
        total = grads_ref[0] + grads_ref[1] + grads_ref[2] + grads_ref[3]
        out_ref[at, :] = base_ref[at, :] - step_size * CODE_FLOOR * total
        return 0

    lax.fori_loop(0, base_ref.shape[0] // rows, piece, 0, unroll=2)


def step_users(z, codes, base, after):
    users, rank = base.shape
    steps = 2
    share = along((users // steps, rank))
    return pl.pallas_call(
        user_kernel,
        out_shape=jax.ShapeDtypeStruct((users, rank), jnp.float32),
        grid_spec=pltpu.PrefetchScalarGridSpec(
            num_scalar_prefetch=1,
            grid=(steps,),
            in_specs=[share] * 5 + [whole(after.shape)],
            out_specs=share,
            scratch_shapes=[pltpu.VMEM((4, 32, rank), jnp.float32)],
        ),
        cost_estimate=pl.CostEstimate(flops=0, bytes_accessed=users * rank * 16, transcendentals=0),
        compiler_params=pltpu.CompilerParams(vmem_limit_bytes=VMEM_LIMIT),
    )(z, *codes, base, after)


def shift(array, axis, j):
    return array if j == 0 else lax.ppermute(array, axis, [(i, (i + j) % 4) for i in range(4)])


def local(user_factors, item_factors, feedback, item_pick, user_noise, item_noise):
    own_index = lax.axis_index(AXES).astype(jnp.int32)
    own = own_index[None]
    z = lax.axis_index("z").astype(jnp.int32)[None]
    tile_size = feedback.shape[2]
    rank_width = item_factors.shape[1]
    held_blocks = item_factors.shape[0] // tile_size
    item_blocks = item_factors.reshape(held_blocks, tile_size, rank_width)
    noise_blocks = item_noise.reshape(held_blocks, tile_size, rank_width)
    user_half = user_factors.astype(jnp.bfloat16)
    to_all = functools.partial(
        lax.all_to_all, axis_name=AXES, split_axis=0, concat_axis=0, tiled=True
    )

    arrived = [to_all(pack(first, own, item_pick, item_blocks)) for first in (True, False)]
    picks, _ = lax.optimization_barrier((item_pick, arrived[0]))
    wanted = lax.dynamic_slice_in_dim(picks, own_index, 1, 1)[:, 0]
    grad, codes = tiles_of(user_half, arrived[0], feedback)
    returned = to_all(codes)
    grad_code, last_codes, base = tiles_of(
        user_half, arrived[1], feedback, grad, user_factors, user_noise
    )
    last_returned = to_all(last_codes)
    grad_codes = [shift(grad_code, "z", j) for j in range(4)]
    new_item = first_settle(z % SEGMENTS, wanted, returned, item_blocks, noise_blocks)
    new_item, done = last_settle(z % SEGMENTS, wanted, last_returned, item_blocks, noise_blocks, new_item)
    new_user = step_users(z, grad_codes, base, done)
    return (new_user, new_item.reshape(item_factors.shape))


def solution(mesh):
    grid = Mesh(mesh.devices.reshape(SIZES), AXES)
    users, items = AXES[:3], AXES
    in_specs = (
        P(users, None),
        P(items, None),
        P("z", users, None),
        P(),
        P(users, None),
        P(items, None),
    )
    out_specs = (P(users, None), P(items, None))
    return jax.shard_map(local, mesh=grid, in_specs=in_specs, out_specs=out_specs, check_vma=False)
```
